256 devices in a mesh: hap: 32 (over z_hi, x, core), mk: 8 (over z_lo, y).
Axes of the slice: x: 4, y: 4, z: 8 (z_hi: 4, z_lo: 2; z = z_hi * 2 + z_lo), core: 2. Of those that a mesh axis runs over, the one named last changes fastest.
Arguments:
- posterior: bfloat16 [40, 1024, 32768], P('mk', None, 'hap'), may hold values from 0 to 1, as said below
- alleles: int32 [32768, 256], P('hap', 'mk'), may hold values from 0 to 1
- owner_map: int32 [1024], replicated, may hold values from 0 to 255, as said below
Outputs:
- dosage: float32 [1024, 256], P(('hap', 'mk'))
The draws below stay inside these ranges and needn't reach their ends.
Inputs may be any that keep to these rules, and one draw needn't show every extreme that they name: `owner_map`: every device index is named by exactly 4 targets. `posterior`: every entry is positive.
All inputs are finite; a program needn't handle non-finite values.
Results may differ from the reference program's by a relative error of at most 0.0003.
Values sent between devices are 32-bit elements; how exact they have to be, the bound alone decides.
No kernel may reach another device: no remote copies, remote signals or barrier semaphores. Data moves between devices by JAX's collectives and lax.ppermute only.
A program may use at most 64 MiB of HBM per device.

```python
import jax
import jax.numpy as jnp
from jax import lax

TGT = 1024
ANCH = 5
MB = 32
MARKERS = 256
REF = 32768
TOWN = 4
N_HAP = 32
N_MK = 8


def draw_owner_map(key, part):
    return (jax.random.permutation(key, TGT) // TOWN).astype(jnp.int32)


def draw_alleles(key, part):
    level_key = jax.random.fold_in(key, 11)
    cell_key = jax.random.fold_in(key, 12)
    level = jax.random.randint(level_key, (1, MARKERS), 1, 1024, dtype=jnp.int32)
    cell = jax.random.randint(cell_key, (REF, MARKERS), 0, 1024, dtype=jnp.int32)
    return (cell < level).astype(jnp.int32)


def draw_posterior(key, part):
    chooser = jax.random.uniform(jax.random.fold_in(key, 21), (ANCH * N_MK, TGT, REF), jnp.float32)
    chance = 16.0 / REF
    peak = 0.25 + 0.74 * (chooser / chance)
    floor_low = jnp.log(1e-05)
    floor_high = jnp.log(0.0001)
    rest = jnp.clip((chooser - chance) / (1.0 - chance), 0.0, 1.0)
    floor = jnp.exp(floor_low + rest * (floor_high - floor_low))
    values = jnp.where(chooser < chance, peak, floor)
    return values.astype(jnp.bfloat16)


def setup_inputs(seed: int = 0) -> dict:
    key_list = jax.random.split(jax.random.key(seed), 4)
    posterior = draw_posterior(jax.random.fold_in(key_list[3], 71), 0)
    alleles = draw_alleles(jax.random.fold_in(key_list[3], 71), 0)
    owner_map = draw_owner_map(jax.random.fold_in(key_list[3], 71), 0)
    return {"posterior": posterior, "alleles": alleles, "owner_map": owner_map}


def interpolate(numerator, denominator):
    anchors = numerator.shape[0]
    intervals = anchors - 1
    block_width = numerator.shape[-1]
    marker_span = block_width // intervals
    ratios = numerator / denominator[:, :, None]
    column = jnp.arange(block_width, dtype=jnp.int32)
    interval = column // marker_span
    weight = ((column % marker_span).astype(jnp.float32) + 0.5) / marker_span
    picker = (interval[None, :] == jnp.arange(intervals, dtype=jnp.int32)[:, None]).astype(jnp.float32)
    left_part = jnp.sum(picker[:, None, :] * ratios[:-1], axis=0)
    right_part = jnp.sum(picker[:, None, :] * ratios[1:], axis=0)
    return (1.0 - weight) * left_part + weight * right_part


def positions(owner_map, devices, per_device):
    owner_table = (owner_map[:, None] == jnp.arange(devices, dtype=jnp.int32)[None, :]).astype(jnp.int32)
    owner_rank = jnp.sum(jnp.cumsum(owner_table, axis=0) * owner_table, axis=1) - 1
    return (owner_map * per_device + owner_rank).astype(jnp.int32)


def reference(posterior, alleles, owner_map):
    allele_bf = alleles.astype(jnp.bfloat16)
    unit_vector = jnp.ones((REF,), jnp.bfloat16)

    def one_anchor(index):
        group = (index // ANCH).astype(jnp.int32)
        matrix = lax.dynamic_index_in_dim(posterior, index, 0, keepdims=False)
        columns = lax.dynamic_slice_in_dim(allele_bf, group * MB, MB, 1)
        top = jnp.dot(matrix, columns, preferred_element_type=jnp.float32)
        bottom = jnp.dot(matrix, unit_vector, preferred_element_type=jnp.float32)
        return top, bottom

    numerator, denominator = lax.map(one_anchor, jnp.arange(ANCH * N_MK, dtype=jnp.int32))
    numerator = numerator.reshape(N_MK, ANCH, TGT, MB)
    denominator = denominator.reshape(N_MK, ANCH, TGT)
    block_dose = jax.vmap(interpolate)(numerator, denominator)
    all_markers = jnp.transpose(block_dose, (1, 0, 2)).reshape(TGT, MARKERS)
    row_of = positions(owner_map, N_HAP * N_MK, TOWN)
    return jnp.zeros((TGT, MARKERS), jnp.float32).at[row_of].set(all_markers)
```

```python
import functools

import jax
import jax.numpy as jnp
from jax import lax
from jax.experimental import pallas as pl
from jax.experimental.pallas import tpu as pltpu
from jax.sharding import Mesh
from jax.sharding import PartitionSpec as P

LANES = 128
CHUNK = 256


def partial_sums(posterior_hbm, alleles_hbm, owner_ref, mine_ref, send_ref,
                 post, allele, weight, place, total, post_sem, allele_sem):
    anchors, targets, haps = post.shape
    block = allele.shape[1]
    span = block // (anchors - 1)
    chunks = targets // CHUNK
    half = mine_ref.shape[0]

    allele_copy = pltpu.make_async_copy(alleles_hbm, allele, allele_sem)
    allele_copy.start()

    def piece(q, k):
        rows = pl.ds(q * CHUNK, CHUNK)
        return pltpu.make_async_copy(
            posterior_hbm.at[k, rows], post.at[k, rows], post_sem.at[q, k])

    for q in range(chunks):
        for k in range(anchors):
            piece(q, k).start()

    core = lax.axis_index("c")
    owner_row = lax.broadcasted_iota(jnp.int32, (CHUNK, CHUNK), 0)
    before = (owner_row < lax.broadcasted_iota(jnp.int32, (CHUNK, CHUNK), 1)).astype(jnp.bfloat16)
    place_row = lax.broadcasted_iota(jnp.int32, (targets, CHUNK), 0)
    seen = jnp.zeros((CHUNK, 1), jnp.float32)
    for q in range(chunks):
        owner = owner_ref[:, pl.ds(q * CHUNK, CHUNK)]
        is_owner = (owner_row == owner).astype(jnp.float32)
        count = seen + jnp.dot(is_owner.astype(jnp.bfloat16), before,
                               preferred_element_type=jnp.float32)
        rank = jnp.sum(is_owner * count, axis=0, keepdims=True).astype(jnp.int32)
        seen = seen + jnp.sum(is_owner, axis=1, keepdims=True)
        other = ((owner >> 3) & 1) ^ core
        row = other * half + ((owner >> 4) * 8 + (owner & 7)) * 4 + rank
        place[:, pl.ds(q * CHUNK, CHUNK)] = (place_row == row).astype(jnp.float32).astype(jnp.bfloat16)

    allele_copy.wait()
    spread_row = lax.broadcasted_iota(jnp.int32, (block, LANES), 0)
    spread_col = lax.broadcasted_iota(jnp.int32, (block, LANES), 1)
    spread = ((spread_col % block == spread_row) & (spread_col < 2 * block)).astype(jnp.bfloat16)
    col = lax.broadcasted_iota(jnp.int32, (1, LANES), 1)
    ones = (col >= 2 * block).astype(jnp.float32)
    filled = jnp.dot(allele[...].astype(jnp.float32).astype(jnp.bfloat16), spread,
                     preferred_element_type=jnp.float32) + ones
    anchor_of = (col % block) // span + (col // block) % 2
    for k in range(anchors):
        weight[k] = (filled * (anchor_of == k).astype(jnp.float32)).astype(jnp.bfloat16)

    for q in range(chunks):
        rows = pl.ds(q * CHUNK, CHUNK)
        sums = None
        for k in range(anchors):
            piece(q, k).wait()
            part = jnp.dot(post[k, rows, :], weight[k], preferred_element_type=jnp.float32)
            sums = part if sums is None else sums + part
        high = sums.astype(jnp.bfloat16)
        low = (sums - high.astype(jnp.float32)).astype(jnp.bfloat16)
        moved = jnp.dot(place[:, rows], jnp.concatenate([high, low], axis=1),
                        preferred_element_type=jnp.float32)
        moved = moved[:, :LANES] + moved[:, LANES:]
        if q == 0:
            total[...] = moved
        elif q < chunks - 1:
            total[...] += moved
        else:
            moved = total[...] + moved
            mine_ref[...] = moved[:half]
            send_ref[...] = moved[half:]


def blend(sums_ref, dose_ref):
    owned = dose_ref.shape[0]
    groups = sums_ref.shape[1] // owned
    block = dose_ref.shape[1] // groups
    total = jnp.sum(sums_ref[...], axis=0)
    ratio = total / pltpu.roll(total, 2 * block, 1)
    col = lax.broadcasted_iota(jnp.int32, (1, LANES), 1)
    w = ((col % 8).astype(jnp.float32) + 0.5) * 0.125
    scaled = ratio * jnp.where(col < block, 1.0 - w, w)
    dose = scaled + pltpu.roll(scaled, LANES - block, 1)
    for g in range(groups):
        dose_ref[:, g * block:(g + 1) * block] = dose[g * owned:(g + 1) * owned, :block]


def on_device(posterior, alleles, owner_map):
    anchors, targets, haps = posterior.shape
    half = targets // 2
    vmem = pl.BlockSpec(memory_space=pltpu.VMEM)
    hbm = pl.BlockSpec(memory_space=pl.ANY)
    mine, send = pl.pallas_call(
        partial_sums,
        out_shape=[jax.ShapeDtypeStruct((half, LANES), jnp.float32)] * 2,
        in_specs=[hbm, hbm, vmem],
        out_specs=[vmem, vmem],
        scratch_shapes=[
            pltpu.VMEM((anchors, targets, haps), jnp.bfloat16),
            pltpu.VMEM(alleles.shape, jnp.int32),
            pltpu.VMEM((anchors, haps, LANES), jnp.bfloat16),
            pltpu.VMEM((targets, targets), jnp.bfloat16),
            pltpu.VMEM((targets, LANES), jnp.float32),
            pltpu.SemaphoreType.DMA((targets // CHUNK, anchors)),
            pltpu.SemaphoreType.DMA,
        ],
        compiler_params=pltpu.CompilerParams(vmem_limit_bytes=40 * 2**20),
    )(posterior, alleles, owner_map.reshape(1, targets))
    got = lax.ppermute(send, "c", [(0, 1), (1, 0)])
    pair = (mine + got).reshape(half // 4, 4, LANES)
    arrived = lax.all_to_all(pair, ("q", "m"), split_axis=0, concat_axis=0, tiled=True)
    markers = alleles.shape[1] * lax.axis_size("m")
    return pl.pallas_call(
        blend,
        out_shape=jax.ShapeDtypeStruct((4, markers), jnp.float32),
        in_specs=[vmem],
        out_specs=vmem,
    )(arrived.reshape(lax.axis_size("q"), half // lax.axis_size("q"), LANES))


def solution(mesh):
    fine = Mesh(mesh.devices.reshape(16, 2, 8), ("q", "c", "m"))
    placed = (P("m", None, ("q", "c")), P(("q", "c"), "m"), P())
    return jax.shard_map(
        on_device, mesh=fine, in_specs=placed, out_specs=P(("q", "c", "m"), None), check_vma=False
    )
```

```python
import functools

import jax
import jax.numpy as jnp
from jax import lax
from jax.experimental import pallas as pl
from jax.experimental.pallas import tpu as pltpu
from jax.sharding import Mesh
from jax.sharding import PartitionSpec as P

LANES = 128
CHUNK = 256
SIZES = (256, 256, 256, 256)
FLIGHT = 2


def partial_sums(posterior_hbm, alleles_hbm, owner_hbm, mine_ref, send_ref,
                 post, allele, owner_ref, weight, place, split, post_sem, allele_sem, owner_sem):
    anchors, targets, haps = post.shape
    block = allele.shape[0]
    span = block // (anchors - 1)
    chunks = targets // CHUNK
    half = mine_ref.shape[0]

    starts = [sum(SIZES[:i]) for i in range(len(SIZES))]

    def piece(i):
        rows = pl.ds(starts[i], SIZES[i])
        return pltpu.make_async_copy(
            posterior_hbm.at[:, rows], post.at[:, rows], post_sem.at[i])

    allele_copy = pltpu.make_async_copy(alleles_hbm, allele, allele_sem)
    owner_copy = pltpu.make_async_copy(owner_hbm, owner_ref, owner_sem)
    owner_copy.start()
    allele_copy.start()
    for i in range(FLIGHT):
        piece(i).start()

    owner_copy.wait()
    core = lax.axis_index("c")
    owner_row = lax.broadcasted_iota(jnp.int32, (CHUNK, CHUNK), 0)
    before = (owner_row < lax.broadcasted_iota(jnp.int32, (CHUNK, CHUNK), 1)).astype(jnp.bfloat16)
    place_row = lax.broadcasted_iota(jnp.int32, (targets, CHUNK), 0)
    seen = jnp.zeros((CHUNK, 1), jnp.float32)
    for q in range(chunks):
        owner = owner_ref[:, pl.ds(q * CHUNK, CHUNK)]
        is_owner = (owner_row == owner).astype(jnp.float32)
        count = seen + jnp.dot(is_owner.astype(jnp.bfloat16), before,
                               preferred_element_type=jnp.float32)
        rank = jnp.sum(is_owner * count, axis=0, keepdims=True).astype(jnp.int32)
        seen = seen + jnp.sum(is_owner, axis=1, keepdims=True)
        other = ((owner >> 3) & 1) ^ core
        row = other * half + ((owner >> 4) * 8 + (owner & 7)) * 4 + rank
        place[:, pl.ds(q * CHUNK, CHUNK)] = (place_row == row).astype(jnp.float32).astype(jnp.bfloat16)

    piece(0).wait()
    piece(FLIGHT).start()
    allele_copy.wait()
    spread_row = lax.broadcasted_iota(jnp.int32, (block, LANES), 0)
    spread_col = lax.broadcasted_iota(jnp.int32, (block, LANES), 1)
    spread = ((spread_col % block == spread_row) & (spread_col < 2 * block)).astype(jnp.bfloat16)
    col = lax.broadcasted_iota(jnp.int32, (1, LANES), 1)
    ones = (col >= 2 * block).astype(jnp.float32)
    filled = lax.dot_general(allele[...].astype(jnp.float32).astype(jnp.bfloat16), spread,
                             (((0,), (0,)), ((), ())), preferred_element_type=jnp.float32) + ones
    anchor_of = (col % block) // span + (col // block) % 2
    for k in range(anchors):
        weight[k] = (filled * (anchor_of == k).astype(jnp.float32)).astype(jnp.bfloat16)

    for i in range(len(SIZES)):
        rows = pl.ds(starts[i], SIZES[i])
        if i > 0:
            piece(i).wait()
            if i + FLIGHT < len(SIZES):
                piece(i + FLIGHT).start()
        sums = jnp.dot(post[0, rows, :], weight[0], preferred_element_type=jnp.float32)
        for k in range(1, anchors):
            sums = sums + jnp.dot(post[k, rows, :], weight[k], preferred_element_type=jnp.float32)
        high = sums.astype(jnp.bfloat16)
        split[rows, :LANES] = high
        split[rows, LANES:] = (sums - high.astype(jnp.float32)).astype(jnp.bfloat16)
    moved = jnp.dot(place[...], split[...], preferred_element_type=jnp.float32)
    moved = moved[:, :LANES] + moved[:, LANES:]
    mine_ref[...] = moved[:half]
    send_ref[...] = moved[half:]


def blend(sums_ref, dose_ref):
    owned = dose_ref.shape[0]
    groups = sums_ref.shape[1] // owned
    block = dose_ref.shape[1] // groups
    total = jnp.sum(sums_ref[...], axis=0)
    ratio = total / pltpu.roll(total, 2 * block, 1)
    col = lax.broadcasted_iota(jnp.int32, (1, LANES), 1)
    w = ((col % 8).astype(jnp.float32) + 0.5) * 0.125
    scaled = ratio * jnp.where(col < block, 1.0 - w, w)
    dose = scaled + pltpu.roll(scaled, LANES - block, 1)
    for g in range(groups):
        dose_ref[:, g * block:(g + 1) * block] = dose[g * owned:(g + 1) * owned, :block]


def on_device(posterior, alleles, owner_map):
    anchors, targets, haps = posterior.shape
    half = targets // 2
    vmem = pl.BlockSpec(memory_space=pltpu.VMEM)
    hbm = pl.BlockSpec(memory_space=pl.ANY)
    mine, send = pl.pallas_call(
        partial_sums,
        out_shape=[jax.ShapeDtypeStruct((half, LANES), jnp.float32)] * 2,
        in_specs=[hbm, hbm, hbm],
        out_specs=[vmem, vmem],
        scratch_shapes=[
            pltpu.VMEM((anchors, targets, haps), jnp.bfloat16),
            pltpu.VMEM(alleles.shape[::-1], jnp.int32),
            pltpu.VMEM((1, targets), jnp.int32),
            pltpu.VMEM((anchors, haps, LANES), jnp.bfloat16),
            pltpu.VMEM((targets, targets), jnp.bfloat16),
            pltpu.VMEM((targets, 2 * LANES), jnp.bfloat16),
            pltpu.SemaphoreType.DMA((len(SIZES),)),
            pltpu.SemaphoreType.DMA,
            pltpu.SemaphoreType.DMA,
        ],
        compiler_params=pltpu.CompilerParams(vmem_limit_bytes=40 * 2**20),
    )(*[pltpu.with_memory_space_constraint(x, pltpu.HBM)
        for x in (posterior, alleles.T, owner_map.reshape(1, targets))])
    got = lax.ppermute(send, "c", [(0, 1), (1, 0)])
    pair = (mine + got).reshape(half // 4, 4, LANES)
    arrived = lax.all_to_all(pair, ("q", "m"), split_axis=0, concat_axis=0, tiled=True)
    markers = alleles.shape[1] * lax.axis_size("m")
    return pl.pallas_call(
        blend,
        out_shape=jax.ShapeDtypeStruct((4, markers), jnp.float32),
        in_specs=[vmem],
        out_specs=vmem,
    )(pltpu.with_memory_space_constraint(
        arrived.reshape(lax.axis_size("q"), half // lax.axis_size("q"), LANES), pltpu.VMEM))


def solution(mesh):
    fine = Mesh(mesh.devices.reshape(16, 2, 8), ("q", "c", "m"))
    placed = (P("m", None, ("q", "c")), P(("q", "c"), "m"), P())
    return jax.shard_map(
        on_device, mesh=fine, in_specs=placed, out_specs=P(("q", "c", "m"), None), check_vma=False
    )
```

```python
import functools

import jax
import jax.numpy as jnp
from jax import lax
from jax.experimental import pallas as pl
from jax.experimental.pallas import tpu as pltpu
from jax.sharding import Mesh
from jax.sharding import PartitionSpec as P

LANES = 128
CHUNK = 256
SIZES = (256, 256, 256, 256)


def partial_sums(posterior_hbm, alleles_hbm, owner_hbm, mine_ref, send_ref,
                 post, allele, owner_ref, weight, place, split, post_sem, allele_sem, owner_sem):
    anchors, targets, haps = post.shape
    block = allele.shape[0]
    span = block // (anchors - 1)
    chunks = targets // CHUNK
    half = mine_ref.shape[0]

    starts = [sum(SIZES[:i]) for i in range(len(SIZES))]

    def piece(i):
        rows = pl.ds(starts[i], SIZES[i])
        return pltpu.make_async_copy(
            posterior_hbm.at[:, rows], post.at[:, rows], post_sem.at[i])

    allele_copy = pltpu.make_async_copy(alleles_hbm, allele, allele_sem)
    owner_copy = pltpu.make_async_copy(owner_hbm, owner_ref, owner_sem)
    owner_copy.start()
    allele_copy.start()
    for i in range(len(SIZES)):
        piece(i).start(priority=1)

    owner_copy.wait()
    core = lax.axis_index("c")
    owner_row = lax.broadcasted_iota(jnp.int32, (CHUNK, CHUNK), 0)
    before = (owner_row < lax.broadcasted_iota(jnp.int32, (CHUNK, CHUNK), 1)).astype(jnp.bfloat16)
    place_row = lax.broadcasted_iota(jnp.int32, (targets, CHUNK), 0)
    seen = jnp.zeros((CHUNK, 1), jnp.float32)
    for q in range(chunks):
        owner = owner_ref[:, pl.ds(q * CHUNK, CHUNK)]
        is_owner = (owner_row == owner).astype(jnp.float32)
        count = seen + jnp.dot(is_owner.astype(jnp.bfloat16), before,
                               preferred_element_type=jnp.float32)
        rank = jnp.sum(is_owner * count, axis=0, keepdims=True).astype(jnp.int32)
        seen = seen + jnp.sum(is_owner, axis=1, keepdims=True)
        other = ((owner >> 3) & 1) ^ core
        row = other * half + ((owner >> 4) * 8 + (owner & 7)) * 4 + rank
        place[:, pl.ds(q * CHUNK, CHUNK)] = (place_row == row).astype(jnp.float32).astype(jnp.bfloat16)

    piece(0).wait()
    allele_copy.wait()
    spread_row = lax.broadcasted_iota(jnp.int32, (block, LANES), 0)
    spread_col = lax.broadcasted_iota(jnp.int32, (block, LANES), 1)
    spread = ((spread_col % block == spread_row) & (spread_col < 2 * block)).astype(jnp.bfloat16)
    col = lax.broadcasted_iota(jnp.int32, (1, LANES), 1)
    ones = (col >= 2 * block).astype(jnp.float32)
    filled = lax.dot_general(allele[...].astype(jnp.float32).astype(jnp.bfloat16), spread,
                             (((0,), (0,)), ((), ())), preferred_element_type=jnp.float32) + ones
    anchor_of = (col % block) // span + (col // block) % 2
    for k in range(anchors):
        weight[k] = (filled * (anchor_of == k).astype(jnp.float32)).astype(jnp.bfloat16)

    for i in range(len(SIZES)):
        rows = pl.ds(starts[i], SIZES[i])
        if i > 0:
            piece(i).wait()
        sums = jnp.dot(post[0, rows, :], weight[0], preferred_element_type=jnp.float32)
        for k in range(1, anchors):
            sums = sums + jnp.dot(post[k, rows, :], weight[k], preferred_element_type=jnp.float32)
        high = sums.astype(jnp.bfloat16)
        split[rows, :LANES] = high
        split[rows, LANES:] = (sums - high.astype(jnp.float32)).astype(jnp.bfloat16)
    moved = jnp.dot(place[...], split[...], preferred_element_type=jnp.float32)
    moved = moved[:, :LANES] + moved[:, LANES:]
    mine_ref[...] = moved[:half]
    send_ref[...] = moved[half:]


def blend(sums_ref, dose_ref):
    owned = dose_ref.shape[0]
    groups = sums_ref.shape[1] // owned
    block = dose_ref.shape[1] // groups
    total = jnp.sum(sums_ref[...], axis=0)
    ratio = total / pltpu.roll(total, 2 * block, 1)
    col = lax.broadcasted_iota(jnp.int32, (1, LANES), 1)
    w = ((col % 8).astype(jnp.float32) + 0.5) * 0.125
    scaled = ratio * jnp.where(col < block, 1.0 - w, w)
    dose = scaled + pltpu.roll(scaled, LANES - block, 1)
    for g in range(groups):
        dose_ref[:, g * block:(g + 1) * block] = dose[g * owned:(g + 1) * owned, :block]


def on_device(posterior, alleles, owner_map):
    anchors, targets, haps = posterior.shape
    half = targets // 2
    vmem = pl.BlockSpec(memory_space=pltpu.VMEM)
    hbm = pl.BlockSpec(memory_space=pl.ANY)
    mine, send = pl.pallas_call(
        partial_sums,
        out_shape=[jax.ShapeDtypeStruct((half, LANES), jnp.float32)] * 2,
        in_specs=[hbm, hbm, hbm],
        out_specs=[vmem, vmem],
        scratch_shapes=[
            pltpu.VMEM((anchors, targets, haps), jnp.bfloat16),
            pltpu.VMEM(alleles.shape[::-1], jnp.int32),
            pltpu.VMEM((1, targets), jnp.int32),
            pltpu.VMEM((anchors, haps, LANES), jnp.bfloat16),
            pltpu.VMEM((targets, targets), jnp.bfloat16),
            pltpu.VMEM((targets, 2 * LANES), jnp.bfloat16),
            pltpu.SemaphoreType.DMA((len(SIZES),)),
            pltpu.SemaphoreType.DMA,
            pltpu.SemaphoreType.DMA,
        ],
        compiler_params=pltpu.CompilerParams(vmem_limit_bytes=40 * 2**20),
    )(*[pltpu.with_memory_space_constraint(x, pltpu.HBM)
        for x in (posterior, alleles.T, owner_map.reshape(1, targets))])
    got = lax.ppermute(send, "c", [(0, 1), (1, 0)])
    pair = (mine + got).reshape(half // 4, 4, LANES)
    arrived = lax.all_to_all(pair, ("q", "m"), split_axis=0, concat_axis=0, tiled=True)
    markers = alleles.shape[1] * lax.axis_size("m")
    return pl.pallas_call(
        blend,
        out_shape=jax.ShapeDtypeStruct((4, markers), jnp.float32),
        in_specs=[vmem],
        out_specs=vmem,
    )(pltpu.with_memory_space_constraint(
        arrived.reshape(lax.axis_size("q"), half // lax.axis_size("q"), LANES), pltpu.VMEM))


def solution(mesh):
    fine = Mesh(mesh.devices.reshape(16, 2, 8), ("q", "c", "m"))
    placed = (P("m", None, ("q", "c")), P(("q", "c"), "m"), P())
    return jax.shard_map(
        on_device, mesh=fine, in_specs=placed, out_specs=P(("q", "c", "m"), None), check_vma=False
    )
```

```python
import functools

import jax
import jax.numpy as jnp
from jax import lax
from jax.experimental import pallas as pl
from jax.experimental.pallas import tpu as pltpu
from jax.sharding import Mesh
from jax.sharding import PartitionSpec as P

LANES = 128
CHUNK = 256
SIZES = (256, 256, 256, 256)


def pack(rows, packed_ref):
    b0, b1, b2, b3 = (rows[i * LANES:(i + 1) * LANES] for i in range(4))
    b1, b2, b3 = pltpu.roll(b1, 96, 1), pltpu.roll(b2, 64, 1), pltpu.roll(b3, 32, 1)
    lane = lax.broadcasted_iota(jnp.int32, b0.shape, 1)
    packed_ref[:, 0, :LANES] = jnp.where(lane < 96, b0, b1)
    packed_ref[:, 0, LANES:2 * LANES] = jnp.where(lane < 64, b1, b2)
    packed_ref[:, 0, 2 * LANES:] = jnp.where(lane < 32, b2, b3)


def partial_sums(posterior_hbm, alleles_hbm, owner_hbm, mine_ref, send_ref,
                 post, allele, owner_ref, weight, place, split, post_sem, allele_sem, owner_sem):
    anchors, targets, haps = post.shape
    block = allele.shape[0]
    span = block // (anchors - 1)
    chunks = targets // CHUNK
    half = targets // 2

    starts = [sum(SIZES[:i]) for i in range(len(SIZES))]

    def piece(i):
        rows = pl.ds(starts[i], SIZES[i])
        return pltpu.make_async_copy(
            posterior_hbm.at[:, rows], post.at[:, rows], post_sem.at[i])

    allele_copy = pltpu.make_async_copy(alleles_hbm, allele, allele_sem)
    owner_copy = pltpu.make_async_copy(owner_hbm, owner_ref, owner_sem)
    owner_copy.start()
    allele_copy.start()
    for i in range(len(SIZES)):
        piece(i).start(priority=1)

    owner_copy.wait()
    core = lax.axis_index("c")
    owner_row = lax.broadcasted_iota(jnp.int32, (CHUNK, CHUNK), 0)
    before = (owner_row < lax.broadcasted_iota(jnp.int32, (CHUNK, CHUNK), 1)).astype(jnp.bfloat16)
    place_row = lax.broadcasted_iota(jnp.int32, (targets, CHUNK), 0)
    seen = jnp.zeros((CHUNK, 1), jnp.float32)
    for q in range(chunks):
        owner = owner_ref[:, pl.ds(q * CHUNK, CHUNK)]
        is_owner = (owner_row == owner).astype(jnp.float32)
        count = seen + jnp.dot(is_owner.astype(jnp.bfloat16), before,
                               preferred_element_type=jnp.float32)
        rank = jnp.sum(is_owner * count, axis=0, keepdims=True).astype(jnp.int32)
        seen = seen + jnp.sum(is_owner, axis=1, keepdims=True)
        other = ((owner >> 3) & 1) ^ core
        row = other * half + rank * LANES + (owner >> 4) * 8 + (owner & 7)
        place[:, pl.ds(q * CHUNK, CHUNK)] = (place_row == row).astype(jnp.float32).astype(jnp.bfloat16)

    piece(0).wait()
    allele_copy.wait()
    spread_row = lax.broadcasted_iota(jnp.int32, (block, LANES), 0)
    spread_col = lax.broadcasted_iota(jnp.int32, (block, LANES), 1)
    spread = ((spread_col % block == spread_row) & (spread_col < 2 * block)).astype(jnp.bfloat16)
    col = lax.broadcasted_iota(jnp.int32, (1, LANES), 1)
    ones = (col >= 2 * block).astype(jnp.float32)
    filled = lax.dot_general(allele[...].astype(jnp.float32).astype(jnp.bfloat16), spread,
                             (((0,), (0,)), ((), ())), preferred_element_type=jnp.float32) + ones
    anchor_of = jnp.where(col < 2 * block, (col % block) // span + col // block, col - 2 * block)
    for k in range(anchors):
        weight[k] = (filled * (anchor_of == k).astype(jnp.float32)).astype(jnp.bfloat16)

    for i in range(len(SIZES)):
        rows = pl.ds(starts[i], SIZES[i])
        if i > 0:
            piece(i).wait()
        sums = jnp.dot(post[0, rows, :], weight[0], preferred_element_type=jnp.float32)
        for k in range(1, anchors):
            sums = sums + jnp.dot(post[k, rows, :], weight[k], preferred_element_type=jnp.float32)
        high = sums.astype(jnp.bfloat16)
        split[rows, :LANES] = high
        split[rows, LANES:] = (sums - high.astype(jnp.float32)).astype(jnp.bfloat16)
    moved = jnp.dot(place[...], split[...], preferred_element_type=jnp.float32)
    moved = moved[:, :LANES] + moved[:, LANES:]
    pack(moved[:half], mine_ref)
    pack(moved[half:], send_ref)


def blend(sums_ref, dose_ref):
    owned = dose_ref.shape[0]
    groups = 8
    block = dose_ref.shape[1] // groups
    parts = sums_ref.shape[0] // groups
    total = sums_ref[:groups, 0, :]
    for part in range(1, parts):
        total = total + sums_ref[part * groups:(part + 1) * groups, 0, :]
    t0, t1, t2 = (total[:, i * LANES:(i + 1) * LANES] for i in range(3))
    lane = lax.broadcasted_iota(jnp.int32, t0.shape, 1)
    rows = jnp.concatenate([
        t0,
        jnp.where(lane < 32, pltpu.roll(t0, 32, 1), pltpu.roll(t1, 32, 1)),
        jnp.where(lane < 64, pltpu.roll(t1, 64, 1), pltpu.roll(t2, 64, 1)),
        pltpu.roll(t2, 96, 1),
    ], axis=0)
    source = lax.broadcasted_iota(jnp.int32, (LANES, LANES), 0) - 2 * block
    col = lax.broadcasted_iota(jnp.int32, (1, LANES), 1)
    anchor_of = (col % block) // 8 + col // block
    pick = ((source == anchor_of) & (col < 2 * block)).astype(jnp.float32)
    below = jnp.dot(rows, pick, precision=lax.Precision.HIGHEST,
                    preferred_element_type=jnp.float32)
    w = ((col % 8).astype(jnp.float32) + 0.5) * 0.125
    scaled = rows / below * jnp.where(col < block, 1.0 - w, w)
    dose = (scaled + pltpu.roll(scaled, LANES - block, 1)).reshape(owned, groups, LANES)
    for g in range(groups):
        dose_ref[:, g * block:(g + 1) * block] = dose[:, g, :block]


def on_device(posterior, alleles, owner_map):
    anchors, targets, haps = posterior.shape
    half = targets // 2
    vmem = pl.BlockSpec(memory_space=pltpu.VMEM)
    hbm = pl.BlockSpec(memory_space=pl.ANY)
    mine, send = pl.pallas_call(
        partial_sums,
        out_shape=[jax.ShapeDtypeStruct((half // 4, 1, 3 * LANES), jnp.float32)] * 2,
        in_specs=[hbm, hbm, hbm],
        out_specs=[vmem, vmem],
        scratch_shapes=[
            pltpu.VMEM((anchors, targets, haps), jnp.bfloat16),
            pltpu.VMEM(alleles.shape[::-1], jnp.int32),
            pltpu.VMEM((1, targets), jnp.int32),
            pltpu.VMEM((anchors, haps, LANES), jnp.bfloat16),
            pltpu.VMEM((targets, targets), jnp.bfloat16),
            pltpu.VMEM((targets, 2 * LANES), jnp.bfloat16),
            pltpu.SemaphoreType.DMA((len(SIZES),)),
            pltpu.SemaphoreType.DMA,
            pltpu.SemaphoreType.DMA,
        ],
        compiler_params=pltpu.CompilerParams(vmem_limit_bytes=40 * 2**20),
    )(*[pltpu.with_memory_space_constraint(x, pltpu.HBM)
        for x in (posterior, alleles.T, owner_map.reshape(1, targets))])
    got = lax.ppermute(send, "c", [(0, 1), (1, 0)])
    pair = mine + got
    arrived = lax.all_to_all(pair, ("q", "m"), split_axis=0, concat_axis=0, tiled=True)
    markers = alleles.shape[1] * lax.axis_size("m")
    return pl.pallas_call(
        blend,
        out_shape=jax.ShapeDtypeStruct((4, markers), jnp.float32),
        in_specs=[vmem],
        out_specs=vmem,
    )(pltpu.with_memory_space_constraint(
        arrived, pltpu.VMEM))


def solution(mesh):
    fine = Mesh(mesh.devices.reshape(16, 2, 8), ("q", "c", "m"))
    placed = (P("m", None, ("q", "c")), P(("q", "c"), "m"), P())
    return jax.shard_map(
        on_device, mesh=fine, in_specs=placed, out_specs=P(("q", "c", "m"), None), check_vma=False
    )
```

```python
import functools

import jax
import jax.numpy as jnp
from jax import lax
from jax.experimental import pallas as pl
from jax.experimental.pallas import tpu as pltpu
from jax.sharding import Mesh
from jax.sharding import PartitionSpec as P

LANES = 128
CHUNK = 256
SIZES = (256, 256, 256, 256)


def pack(rows, packed_ref):
    b0, b1, b2, b3 = (rows[i * LANES:(i + 1) * LANES] for i in range(4))
    b1, b2, b3 = pltpu.roll(b1, 96, 1), pltpu.roll(b2, 64, 1), pltpu.roll(b3, 32, 1)
    lane = lax.broadcasted_iota(jnp.int32, b0.shape, 1)
    packed_ref[:, 0, :LANES] = jnp.where(lane < 96, b0, b1)
    packed_ref[:, 0, LANES:2 * LANES] = jnp.where(lane < 64, b1, b2)
    packed_ref[:, 0, 2 * LANES:] = jnp.where(lane < 32, b2, b3)


def partial_sums(posterior_hbm, alleles_hbm, owner_hbm, mine_ref, send_ref,
                 post, allele, owner_ref, weight, place, split, post_sem, allele_sem, owner_sem):
    anchors, targets, haps = post.shape
    block = allele.shape[0]
    span = block // (anchors - 1)
    chunks = targets // CHUNK
    half = targets // 2

    starts = [sum(SIZES[:i]) for i in range(len(SIZES))]

    def piece(i):
        rows = pl.ds(starts[i], SIZES[i])
        return pltpu.make_async_copy(
            posterior_hbm.at[:, rows], post.at[:, rows], post_sem.at[i])

    allele_copy = pltpu.make_async_copy(alleles_hbm, allele, allele_sem)
    owner_copy = pltpu.make_async_copy(owner_hbm, owner_ref, owner_sem)
    owner_copy.start()
    allele_copy.start()
    for i in range(len(SIZES)):
        piece(i).start(priority=1)

    owner_copy.wait()
    core = lax.axis_index("c")
    owner_row = lax.broadcasted_iota(jnp.int32, (CHUNK, CHUNK), 0)
    before = (owner_row < lax.broadcasted_iota(jnp.int32, (CHUNK, CHUNK), 1)).astype(jnp.bfloat16)
    place_row = lax.broadcasted_iota(jnp.int32, (targets, CHUNK), 0)
    seen = jnp.zeros((CHUNK, 1), jnp.float32)
    for q in range(chunks):
        owner = owner_ref[:, pl.ds(q * CHUNK, CHUNK)]
        is_owner = (owner_row == owner).astype(jnp.float32)
        count = seen + jnp.dot(is_owner.astype(jnp.bfloat16), before,
                               preferred_element_type=jnp.float32)
        rank = jnp.sum(is_owner * count, axis=0, keepdims=True).astype(jnp.int32)
        seen = seen + jnp.sum(is_owner, axis=1, keepdims=True)
        other = ((owner >> 3) & 1) ^ core
        row = other * half + rank * LANES + (owner & 7) * 16 + (owner >> 4)
        place[:, pl.ds(q * CHUNK, CHUNK)] = (place_row == row).astype(jnp.float32).astype(jnp.bfloat16)

    piece(0).wait()
    allele_copy.wait()
    spread_row = lax.broadcasted_iota(jnp.int32, (block, LANES), 0)
    spread_col = lax.broadcasted_iota(jnp.int32, (block, LANES), 1)
    spread = ((spread_col % block == spread_row) & (spread_col < 2 * block)).astype(jnp.bfloat16)
    col = lax.broadcasted_iota(jnp.int32, (1, LANES), 1)
    ones = (col >= 2 * block).astype(jnp.float32)
    filled = lax.dot_general(allele[...].astype(jnp.float32).astype(jnp.bfloat16), spread,
                             (((0,), (0,)), ((), ())), preferred_element_type=jnp.float32) + ones
    anchor_of = jnp.where(col < 2 * block, (col % block) // span + col // block, col - 2 * block)
    for k in range(anchors):
        weight[k] = (filled * (anchor_of == k).astype(jnp.float32)).astype(jnp.bfloat16)

    for i in range(len(SIZES)):
        rows = pl.ds(starts[i], SIZES[i])
        if i > 0:
            piece(i).wait()
        sums = jnp.dot(post[0, rows, :], weight[0], preferred_element_type=jnp.float32)
        for k in range(1, anchors):
            sums = sums + jnp.dot(post[k, rows, :], weight[k], preferred_element_type=jnp.float32)
        high = sums.astype(jnp.bfloat16)
        split[rows, :LANES] = high
        split[rows, LANES:] = (sums - high.astype(jnp.float32)).astype(jnp.bfloat16)
    moved = jnp.dot(place[...], split[...], preferred_element_type=jnp.float32)
    moved = moved[:, :LANES] + moved[:, LANES:]
    pack(moved[:half], mine_ref)
    pack(moved[half:], send_ref)


def blend(sums_ref, dose_ref):
    owned = dose_ref.shape[0]
    groups = 8
    block = dose_ref.shape[1] // groups
    parts = sums_ref.shape[0] // groups
    total = jnp.sum(sums_ref[:, 0, :].reshape(groups, parts, 3 * LANES), axis=1)
    t0, t1, t2 = (total[:, i * LANES:(i + 1) * LANES] for i in range(3))
    lane = lax.broadcasted_iota(jnp.int32, t0.shape, 1)
    rows = jnp.concatenate([
        t0,
        jnp.where(lane < 32, pltpu.roll(t0, 32, 1), pltpu.roll(t1, 32, 1)),
        jnp.where(lane < 64, pltpu.roll(t1, 64, 1), pltpu.roll(t2, 64, 1)),
        pltpu.roll(t2, 96, 1),
    ], axis=0)
    source = lax.broadcasted_iota(jnp.int32, (LANES, LANES), 0) - 2 * block
    col = lax.broadcasted_iota(jnp.int32, (1, LANES), 1)
    anchor_of = (col % block) // 8 + col // block
    pick = ((source == anchor_of) & (col < 2 * block)).astype(jnp.float32)
    below = jnp.dot(rows, pick, precision=lax.Precision.HIGHEST,
                    preferred_element_type=jnp.float32)
    w = ((col % 8).astype(jnp.float32) + 0.5) * 0.125
    scaled = rows / below * jnp.where(col < block, 1.0 - w, w)
    dose = (scaled + pltpu.roll(scaled, LANES - block, 1)).reshape(owned, groups, LANES)
    for g in range(groups):
        dose_ref[:, g * block:(g + 1) * block] = dose[:, g, :block]


def on_device(posterior, alleles, owner_map):
    anchors, targets, haps = posterior.shape
    half = targets // 2
    vmem = pl.BlockSpec(memory_space=pltpu.VMEM)
    hbm = pl.BlockSpec(memory_space=pl.ANY)
    mine, send = pl.pallas_call(
        partial_sums,
        out_shape=[jax.ShapeDtypeStruct((half // 4, 1, 3 * LANES), jnp.float32)] * 2,
        in_specs=[hbm, hbm, hbm],
        out_specs=[vmem, vmem],
        scratch_shapes=[
            pltpu.VMEM((anchors, targets, haps), jnp.bfloat16),
            pltpu.VMEM(alleles.shape[::-1], jnp.int32),
            pltpu.VMEM((1, targets), jnp.int32),
            pltpu.VMEM((anchors, haps, LANES), jnp.bfloat16),
            pltpu.VMEM((targets, targets), jnp.bfloat16),
            pltpu.VMEM((targets, 2 * LANES), jnp.bfloat16),
            pltpu.SemaphoreType.DMA((len(SIZES),)),
            pltpu.SemaphoreType.DMA,
            pltpu.SemaphoreType.DMA,
        ],
        compiler_params=pltpu.CompilerParams(vmem_limit_bytes=40 * 2**20),
    )(*[pltpu.with_memory_space_constraint(x, pltpu.HBM)
        for x in (posterior, alleles.T, owner_map.reshape(1, targets))])
    got = lax.ppermute(send, "c", [(0, 1), (1, 0)])
    pair = mine + got
    arrived = lax.all_to_all(pair, ("m", "q"), split_axis=0, concat_axis=0, tiled=True)
    markers = alleles.shape[1] * lax.axis_size("m")
    return pl.pallas_call(
        blend,
        out_shape=jax.ShapeDtypeStruct((4, markers), jnp.float32),
        in_specs=[vmem],
        out_specs=vmem,
    )(pltpu.with_memory_space_constraint(
        arrived, pltpu.VMEM))


def solution(mesh):
    fine = Mesh(mesh.devices.reshape(16, 2, 8), ("q", "c", "m"))
    placed = (P("m", None, ("q", "c")), P(("q", "c"), "m"), P())
    return jax.shard_map(
        on_device, mesh=fine, in_specs=placed, out_specs=P(("q", "c", "m"), None), check_vma=False
    )
```
